512 devices in a mesh: ctx: 64 (over z, y_lo, core), head: 8 (over y_hi, x).
Axes of the slice: x: 4, y: 4 (y_hi: 2, y_lo: 2; y = y_hi * 2 + y_lo), z: 16, core: 2. Of those that a mesh axis runs over, the one named last changes fastest.
Arguments:
- queries: float32 [16384, 32, 128], P(('ctx', 'head')), may hold values from -6.1 to 6.1
- keys: float32 [16384, 16, 128], P(('ctx', 'head')), may hold values from -6.1 to 6.1
- values: float32 [16384, 16, 128], P(('ctx', 'head')), may hold values from -6 to 6
- out_grad: float32 [16384, 32, 128], P(('ctx', 'head')), may hold values from -6 to 6
Outputs:
- attention: float32 [16384, 32, 128], P(('ctx', 'head'))
- query_grad: float32 [16384, 32, 128], P(('ctx', 'head'))
- key_grad: float32 [16384, 16, 128], P(('ctx', 'head'))
- value_grad: float32 [16384, 16, 128], P(('ctx', 'head'))
The draws below stay inside these ranges and needn't reach their ends.
All inputs are finite; a program needn't handle non-finite values.
Results may differ from the reference program's by a relative error of at most 0.0003.
Values sent between devices are 32-bit elements; how exact they have to be, the bound alone decides.
No kernel may reach another device: no remote copies, remote signals or barrier semaphores. Data moves between devices by JAX's collectives and lax.ppermute only.
A program may use at most 64 MiB of HBM per device.

```python
import jax
import jax.numpy as jnp
from jax import lax

HEADS = 32
KV_HEADS = 16
HEAD_DIM = 128
WINDOW = 1024
TOK_DEV = 256
TOKENS = 16384


def draw_queries(key, part):
    noise_key = jax.random.fold_in(key, 11)
    return jnp.clip(jax.random.normal(noise_key, (TOKENS, HEADS, HEAD_DIM)), -6.0, 6.0).astype(jnp.float32)


def draw_keys(key, part):
    noise_key = jax.random.fold_in(key, 21)
    return jnp.clip(jax.random.normal(noise_key, (TOKENS, KV_HEADS, HEAD_DIM)), -6.0, 6.0).astype(jnp.float32)


def level_of(key, dims, shards, smallest, high):
    factor_of, own = 1.0, jax.random.fold_in(key, 6)
    for dim, shards_of in shards:
        steps = jnp.exp(jax.random.uniform(jax.random.fold_in(own, dim), (shards_of,), jnp.float32, smallest / len(shards), high / len(shards)))
        factor_of = factor_of * jnp.repeat(steps, dims[dim] // shards_of).reshape([-1 if axis == dim else 1 for axis in range(len(dims))])
    return factor_of


def normal_values(own_key, extent, width, reach, cuts=(), kind=jnp.bfloat16):
    entries = jax.random.normal(own_key, extent, jnp.float32) * width
    if len(cuts) > 0:
        entries = level_of(own_key, extent, cuts, -0.22, 0.18) * entries
    return jnp.clip(entries, min=-reach, max=reach).astype(kind)


def setup_inputs(seed: int = 0) -> dict:
    seeds = jax.random.split(jax.random.key(seed), 5)
    queries = draw_queries(jax.random.fold_in(seeds[4], 71), 0)
    keys = draw_keys(jax.random.fold_in(seeds[4], 71), 0)
    values = normal_values(seeds[2], (TOKENS, KV_HEADS, HEAD_DIM), 1.0, 6.0, ((0, 512),), jnp.float32)
    out_grad = normal_values(seeds[3], (TOKENS, HEADS, HEAD_DIM), 1.0, 6.0, ((0, 512),), jnp.float32)
    return {"queries": queries, "keys": keys, "values": values, "out_grad": out_grad}


query_scale = 168.0 ** -0.5
highest = lax.Precision.HIGHEST


def attend(query_rows, grad_rows, key_rows, value_rows, anchor):
    row_count, head_count, head_dim = query_rows.shape
    groups = key_rows.shape[1]
    group_size = head_count // groups
    key_count = key_rows.shape[0]
    grouped = query_rows.reshape(row_count, groups, group_size, head_dim)
    grad_grouped = grad_rows.reshape(row_count, groups, group_size, head_dim)
    scores = jnp.einsum("rgeh,cgh->gerc", grouped, key_rows, precision=highest) * query_scale
    row_iota = lax.broadcasted_iota(jnp.int32, (row_count, key_count), 0)
    col_iota = lax.broadcasted_iota(jnp.int32, (row_count, key_count), 1)
    offset = row_iota - col_iota + WINDOW
    position = anchor - WINDOW + col_iota
    allowed = (offset >= 0) & (offset < WINDOW) & (position >= 0)
    row_max = jnp.max(jnp.where(allowed, scores, -jnp.inf), axis=-1, keepdims=True)
    weights = jnp.exp(jnp.where(allowed, scores - row_max, -jnp.inf))
    normed = weights / jnp.sum(weights, axis=-1, keepdims=True)
    attention = jnp.einsum("gerc,cgh->rgeh", normed, value_rows, precision=highest)
    row_dots = jnp.transpose(jnp.sum(grad_grouped * attention, axis=-1), (1, 2, 0))[..., None]
    prob_grad = jnp.einsum("rgeh,cgh->gerc", grad_grouped, value_rows, precision=highest)
    score_grad = normed * (prob_grad - row_dots)
    query_grad = jnp.einsum("gerc,cgh->rgeh", score_grad, key_rows, precision=highest) * query_scale
    key_grad = jnp.einsum("gerc,rgeh->cgh", score_grad, grouped, precision=highest) * query_scale
    value_grad = jnp.einsum("gerc,rgeh->cgh", normed, grad_grouped, precision=highest)
    shape_out = (row_count, head_count, head_dim)
    return attention.reshape(shape_out), query_grad.reshape(shape_out), key_grad, value_grad


def reference(queries, keys, values, out_grad):
    total_rows = queries.shape[0]
    block_len = min(TOK_DEV, 256)
    blocks = total_rows // block_len
    padding = jnp.zeros((WINDOW,) + keys.shape[1:], keys.dtype)
    keys_padded = jnp.concatenate([padding, keys], axis=0)
    values_padded = jnp.concatenate([padding, values], axis=0)

    def visit(accum, block_index):
        key_sums, value_sums = accum
        start_row = (block_index * block_len).astype(jnp.int32)
        query_rows = lax.dynamic_slice_in_dim(queries, start_row, block_len, 0)
        grad_rows = lax.dynamic_slice_in_dim(out_grad, start_row, block_len, 0)
        key_rows = lax.dynamic_slice_in_dim(keys_padded, start_row, WINDOW + block_len, 0)
        value_rows = lax.dynamic_slice_in_dim(values_padded, start_row, WINDOW + block_len, 0)
        attention, query_grad, key_grad, value_grad = attend(query_rows, grad_rows, key_rows, value_rows, start_row)
        earlier_keys = lax.dynamic_slice_in_dim(key_sums, start_row, WINDOW + block_len, 0)
        earlier_values = lax.dynamic_slice_in_dim(value_sums, start_row, WINDOW + block_len, 0)
        key_sums = lax.dynamic_update_slice_in_dim(key_sums, earlier_keys + key_grad, start_row, 0)
        value_sums = lax.dynamic_update_slice_in_dim(value_sums, earlier_values + value_grad, start_row, 0)
        return (key_sums, value_sums), (attention, query_grad)

    starting = jnp.zeros((total_rows + WINDOW,) + keys.shape[1:], keys.dtype)
    (key_sums, value_sums), (attn_blocks, qgrad_blocks) = lax.scan(visit, (starting, starting), jnp.arange(blocks, dtype=jnp.int32))
    return (attn_blocks.reshape(queries.shape), qgrad_blocks.reshape(queries.shape), key_sums[WINDOW:], value_sums[WINDOW:])
```

```python
import jax
import jax.numpy as jnp
from jax import lax
from jax.experimental import pallas as pl
from jax.experimental.pallas import tpu as pltpu
from jax.sharding import Mesh, PartitionSpec as P

WINDOW = 1024
HEADS = 32
GROUPS = 16
HEAD_DIM = 128
ROWS = 32
BLOCK = 256
PEERS = 16
PLANE_AXES = ("ylo", "head")

query_scale = 168.0 ** (-0.5)
f32 = jnp.float32
bf16 = jnp.bfloat16

VMEM = pl.BlockSpec(memory_space=pltpu.VMEM)


def params():
    return pltpu.CompilerParams(vmem_limit_bytes=40 * 1024 * 1024)


def pack_kv_kernel(k_ref, v_ref, out_ref):
    for g in range(GROUPS):
        out_ref[g, 0] = k_ref[:, g, :]
        out_ref[g, 1] = v_ref[:, g, :]


def pack_q_kernel(q_ref, d_ref, out_ref):
    for g in range(GROUPS):
        for h in range(2):
            out_ref[g, h] = q_ref[:, 2 * g + h, :]
            out_ref[g, 2 + h] = d_ref[:, 2 * g + h, :]


def unpack_kv_kernel(in_ref, k_ref, v_ref):
    for g in range(GROUPS):
        k_ref[:, g, :] = in_ref[g, 0]
        v_ref[:, g, :] = in_ref[g, 1]


def unpack_q_kernel(in_ref, a_ref, q_ref):
    for g in range(GROUPS):
        for h in range(2):
            a_ref[:, 2 * g + h, :] = in_ref[g, h]
            q_ref[:, 2 * g + h, :] = in_ref[g, 2 + h]


def split(x):
    hi = x.astype(bf16)
    lo = (x - hi.astype(f32)).astype(bf16)
    return hi, lo


def dot(a, b):
    return lax.dot_general(a, b, (((1,), (0,)), ((), ())), preferred_element_type=f32)


def attend_kernel(
    q_ref, own_ref, ownx_ref, halo_ref, halox_ref,
    out_ref, gown_ref, gownx_ref, ghalo_ref, ghalox_ref,
    kcat, vcat, kt, vt, s_ref, w_hi, w_lo, dk, dv,
):
    z = lax.axis_index("z")
    core = lax.axis_index("core")
    other = 1 - core
    for base, mine, ref in ((0, core, halo_ref), (0, other, halox_ref), (4, core, own_ref), (4, other, ownx_ref)):
        for y in range(2):
            at = base + 2 * y + mine
            rows = pl.ds(pl.multiple_of(at * BLOCK, BLOCK), BLOCK)
            for i, cat, tr in ((0, kcat, kt), (1, vcat, vt)):
                x = ref[8 * y : 8 * y + 8, i].reshape(BLOCK, HEAD_DIM)
                hi, lo = split(x)
                cat[rows, :HEAD_DIM] = hi
                cat[rows, HEAD_DIM:] = lo
                thi, tlo = split(x.T)
                tr[at, :HEAD_DIM, :] = thi
                tr[at, HEAD_DIM:, :] = tlo
    dk[...] = jnp.zeros_like(dk)
    dv[...] = jnp.zeros_like(dv)
    key_iota = lax.broadcasted_iota(jnp.int32, (BLOCK, BLOCK), 0)
    query_iota = lax.broadcasted_iota(jnp.int32, (BLOCK, BLOCK), 1)
    for y in range(2):
        first = 2 * y + core
        for h in range(2):
            q = q_ref[8 * y : 8 * y + 8, h].reshape(BLOCK, HEAD_DIM) * query_scale
            d = q_ref[8 * y : 8 * y + 8, 2 + h].reshape(BLOCK, HEAD_DIM)
            q_hi, q_lo = split(q)
            qcat = jnp.concatenate([q_hi, q_lo], axis=1)
            qt_hi, qt_lo = split(q.T)
            qt2 = jnp.concatenate([qt_hi, qt_hi], axis=0)
            dt = d.T
            maxes = []
            for b in range(5):
                rows = pl.ds(pl.multiple_of((first + b) * BLOCK, BLOCK), BLOCK)
                s = dot(kcat[rows, :], qt2) + dot(kcat[rows, :HEAD_DIM], qt_lo)
                if b == 0:
                    s = jnp.where(key_iota > query_iota, s, -jnp.inf)
                if b == 4:
                    s = jnp.where(key_iota <= query_iota, s, -jnp.inf)
                s_ref[b] = s
                m = jnp.max(s, axis=0, keepdims=True)
                exists = (z * 4 + first + b - 4) >= 0
                maxes.append(jnp.where(exists, m, -jnp.inf))
            row_max = maxes[4]
            for b in range(4):
                row_max = jnp.maximum(row_max, maxes[b])
            total = jnp.zeros((1, BLOCK), f32)
            at_sum = jnp.zeros((HEAD_DIM, BLOCK), f32)
            for b in range(5):
                exists = (z * 4 + first + b - 4) >= 0
                shift = jnp.where(exists, row_max, jnp.inf)
                w = jnp.exp(s_ref[b] - shift)
                total = total + jnp.sum(w, axis=0, keepdims=True)
                hi, lo = split(w)
                s_ref[b] = w
                w_hi[b] = hi
                w_lo[b] = lo
                vtb = vt[first + b]
                both = dot(vtb, hi)
                at_sum = at_sum + (both[:HEAD_DIM] + both[HEAD_DIM:] + dot(vtb[:HEAD_DIM], lo))
            inverse = 1.0 / total
            at_sum = at_sum * inverse
            out_ref[8 * y : 8 * y + 8, h] = at_sum.T.reshape(8, ROWS, HEAD_DIM)
            dt = dt * inverse
            row_dots = jnp.sum(dt * at_sum, axis=0, keepdims=True)
            dt_hi, dt_lo = split(dt)
            dt2 = jnp.concatenate([dt_hi, dt_hi], axis=0)
            d_hi, d_lo = split(dt.T)
            dcat = jnp.concatenate([d_hi, d_lo], axis=1)
            dq_sum = jnp.zeros((HEAD_DIM, BLOCK), f32)
            for b in range(5):
                rows = pl.ds(pl.multiple_of((first + b) * BLOCK, BLOCK), BLOCK)
                both = dot(w_hi[b], dcat)
                dv[rows, :] += both[:, :HEAD_DIM] + both[:, HEAD_DIM:] + dot(w_lo[b], d_hi)
                dp = dot(vcat[rows, :], dt2) + dot(vcat[rows, :HEAD_DIM], dt_lo)
                hi, lo = split(s_ref[b] * (dp - row_dots))
                ktb = kt[first + b]
                both = dot(ktb, hi)
                dq_sum = dq_sum + (both[:HEAD_DIM] + both[HEAD_DIM:] + dot(ktb[:HEAD_DIM], lo))
                both = dot(hi, qcat)
                dk[rows, :] += both[:, :HEAD_DIM] + both[:, HEAD_DIM:] + dot(lo, q_hi)
            dq_sum = dq_sum * query_scale
            out_ref[8 * y : 8 * y + 8, 2 + h] = dq_sum.T.reshape(8, ROWS, HEAD_DIM)
    for base, mine, ref in ((0, core, ghalo_ref), (0, other, ghalox_ref), (4, core, gown_ref), (4, other, gownx_ref)):
        for y in range(2):
            rows = pl.ds(pl.multiple_of((base + 2 * y + mine) * BLOCK, BLOCK), BLOCK)
            ref[8 * y : 8 * y + 8, 0] = dk[rows, :].reshape(8, ROWS, HEAD_DIM)
            ref[8 * y : 8 * y + 8, 1] = dv[rows, :].reshape(8, ROWS, HEAD_DIM)


def shape(*dims):
    return jax.ShapeDtypeStruct(dims, f32)


def call(kernel, outs, ins, scratch=()):
    return pl.pallas_call(
        kernel,
        out_shape=outs,
        in_specs=[VMEM] * len(ins),
        out_specs=[VMEM] * len(outs) if isinstance(outs, tuple) else VMEM,
        scratch_shapes=list(scratch),
        compiler_params=params(),
    )(*ins)


def exchanged(x):
    return lax.all_to_all(x, PLANE_AXES, 0, 0, tiled=True)


def swapped(x):
    return lax.ppermute(x, "core", [(0, 1), (1, 0)])


def per_device(queries, keys, values, out_grad):
    planes = lax.axis_size("z")
    kv_shape = shape(PEERS, 2, ROWS, HEAD_DIM)
    q_shape = shape(PEERS, 4, ROWS, HEAD_DIM)
    own = exchanged(call(pack_kv_kernel, kv_shape, (keys, values)))
    rows = exchanged(call(pack_q_kernel, q_shape, (queries, out_grad)))
    halo = lax.ppermute(own, "z", [(i, i + 1) for i in range(planes - 1)])
    ownx = swapped(own)
    halox = swapped(halo)
    scratch = (
        pltpu.VMEM((8 * BLOCK, 2 * HEAD_DIM), bf16),
        pltpu.VMEM((8 * BLOCK, 2 * HEAD_DIM), bf16),
        pltpu.VMEM((8, 2 * HEAD_DIM, BLOCK), bf16),
        pltpu.VMEM((8, 2 * HEAD_DIM, BLOCK), bf16),
        pltpu.VMEM((5, BLOCK, BLOCK), f32),
        pltpu.VMEM((5, BLOCK, BLOCK), bf16),
        pltpu.VMEM((5, BLOCK, BLOCK), bf16),
        pltpu.VMEM((8 * BLOCK, HEAD_DIM), f32),
        pltpu.VMEM((8 * BLOCK, HEAD_DIM), f32),
    )
    out, gown, gownx, ghalo, ghalox = call(
        attend_kernel, (q_shape, kv_shape, kv_shape, kv_shape, kv_shape), (rows, own, ownx, halo, halox), scratch
    )
    back = exchanged(out)
    ghalo = ghalo + swapped(ghalox)
    returned = lax.ppermute(ghalo, "z", [(i + 1, i) for i in range(planes - 1)])
    total = gown + swapped(gownx) + returned
    kv_back = exchanged(total)
    attention, query_grad = call(unpack_q_kernel, (shape(ROWS, HEADS, HEAD_DIM),) * 2, (back,))
    key_grad, value_grad = call(unpack_kv_kernel, (shape(ROWS, GROUPS, HEAD_DIM),) * 2, (kv_back,))
    return attention, query_grad, key_grad, value_grad


def solution(mesh):
    inner = Mesh(mesh.devices.reshape(-1, 2, 2, mesh.shape["head"]), ("z", "ylo", "core", "head"))
    spec = P(("z", "ylo", "core", "head"), None, None)
    return jax.shard_map(per_device, mesh=inner, in_specs=(spec,) * 4, out_specs=(spec,) * 4, check_vma=False)
```

```python
import jax
import jax.numpy as jnp
from jax import lax
from jax.experimental import pallas as pl
from jax.experimental.pallas import tpu as pltpu
from jax.sharding import Mesh, PartitionSpec as P

WINDOW = 1024
HEADS = 32
GROUPS = 16
HEAD_DIM = 128
ROWS = 32
BLOCK = 256
PEERS = 16
PLANE_AXES = ("ylo", "head")

query_scale = 168.0 ** (-0.5)
LOG2E = 1.4426950408889634
LN2 = 0.6931471805599453
f32 = jnp.float32
bf16 = jnp.bfloat16

VMEM = pl.BlockSpec(memory_space=pltpu.VMEM)


def params(vmem):
    return pltpu.CompilerParams(vmem_limit_bytes=vmem * 1024 * 1024)


def pack_kv_kernel(k_ref, v_ref, out_ref):
    for g in range(GROUPS):
        out_ref[g, 0] = k_ref[:, g, :]
        out_ref[g, 1] = v_ref[:, g, :]


def pack_q_kernel(q_ref, d_ref, out_ref):
    for g in range(GROUPS):
        for h in range(2):
            out_ref[g, h] = q_ref[:, 2 * g + h, :]
            out_ref[g, 2 + h] = d_ref[:, 2 * g + h, :]


def unpack_kv_kernel(in_ref, k_ref, v_ref):
    for g in range(GROUPS):
        k_ref[:, g, :] = in_ref[g, 0]
        v_ref[:, g, :] = in_ref[g, 1]


def unpack_q_kernel(in_ref, a_ref, q_ref):
    for g in range(GROUPS):
        for h in range(2):
            a_ref[:, 2 * g + h, :] = in_ref[g, h]
            q_ref[:, 2 * g + h, :] = in_ref[g, 2 + h]


def split(x):
    hi = x.astype(bf16)
    lo = (x - hi.astype(f32)).astype(bf16)
    return hi, lo


def dot(a, b):
    return lax.dot_general(a, b, (((1,), (0,)), ((), ())), preferred_element_type=f32)


SPAN = 5 * BLOCK


def attend_kernel(
    rows_in, own_in, halo_in, other_in,
    out_buf, gmine, gother,
    kcat, vcat, kt, vt, s_ref, wcat, dscat, qw_ref, dw_ref,
):
    z = lax.axis_index("z")
    core = lax.axis_index("core")
    for r in range(7):
        here = pl.ds(r * BLOCK, BLOCK)
        for i, cat, tr in ((0, kcat, kt), (1, vcat, vt)):
            ref, at = (other_in, 8 * (r // 2)) if r % 2 else (halo_in if r < 4 else own_in, 8 * (r // 2 % 2))
            x = ref[at : at + 8, i]
            x = x.reshape(BLOCK, HEAD_DIM)
            hi, lo = split(x)
            cat[here, :HEAD_DIM] = hi
            cat[here, HEAD_DIM : 2 * HEAD_DIM] = lo
            cat[here, 2 * HEAD_DIM :] = hi
            thi, tlo = split(x.T)
            tr[:HEAD_DIM, here] = thi
            tr[HEAD_DIM:, here] = tlo
    key_iota = lax.broadcasted_iota(jnp.int32, (BLOCK, BLOCK), 0)
    query_iota = lax.broadcasted_iota(jnp.int32, (BLOCK, BLOCK), 1)
    later = key_iota > query_iota

    def exists(y, b):
        return (z * 4 + 2 * y + core + b - 4) >= 0

    state = {}

    def scores(y, h):
        q = rows_in[8 * y : 8 * y + 8, h].reshape(BLOCK, HEAD_DIM) * (query_scale * LOG2E)
        qt_hi, qt_lo = split(q.T)
        q_hi, q_lo = split(q)
        qt3 = jnp.concatenate([qt_hi, qt_hi, qt_lo], axis=0)
        row_max = None
        for b in range(5):
            here = pl.ds((2 * y + b) * BLOCK, BLOCK)
            s = dot(kcat[here, :], qt3)
            if b == 0:
                s = jnp.where(later, s, -jnp.inf)
            if b == 4:
                s = jnp.where(later, -jnp.inf, s)
            s_ref[2 * y + h, b] = s
            m = jnp.max(s, axis=0, keepdims=True)
            if b < 4:
                m = jnp.where(exists(y, b), m, -jnp.inf)
            row_max = m if row_max is None else jnp.maximum(row_max, m)
        qw_ref[y, h * BLOCK : (h + 1) * BLOCK, :] = jnp.concatenate([q_hi, q_lo], axis=1)
        state[y, h] = row_max

    def weigh(y, h):
        row_max = state[y, h]
        i = 2 * y + h
        total = None
        for b in range(5):
            shift = row_max if b == 4 else jnp.where(exists(y, b), row_max, jnp.inf)
            w = jnp.exp2(s_ref[i, b] - shift)
            t = jnp.sum(w, axis=0, keepdims=True)
            total = t if total is None else total + t
            hi, lo = split(w)
            s_ref[i, b] = w
            wcat[y, b * BLOCK : (b + 1) * BLOCK, h * 512 : h * 512 + 256] = hi
            wcat[y, b * BLOCK : (b + 1) * BLOCK, h * 512 + 256 : h * 512 + 512] = lo
        vts = vt[:, 2 * y * BLOCK : 2 * y * BLOCK + SPAN]
        both = dot(vts, wcat[y, :, h * 512 : h * 512 + 256])
        at_sum = both[:HEAD_DIM] + both[HEAD_DIM:] + dot(vts[:HEAD_DIM], wcat[y, :, h * 512 + 256 : h * 512 + 512])
        inverse = 1.0 / total
        at_sum = at_sum * inverse
        out_buf[8 * y : 8 * y + 8, h] = at_sum.T.reshape(8, ROWS, HEAD_DIM)
        dt = rows_in[8 * y : 8 * y + 8, 2 + h].reshape(BLOCK, HEAD_DIM).T * inverse
        row_dots = jnp.sum(dt * at_sum, axis=0, keepdims=True)
        d_hi, d_lo = split(dt.T)
        dw_ref[y, h * BLOCK : (h + 1) * BLOCK, :] = jnp.concatenate([d_hi, d_lo], axis=1)
        state[y, h] = (row_dots, dt)

    def grads(y, h):
        row_dots, dt = state[y, h]
        i = 2 * y + h
        dt_hi, dt_lo = split(dt)
        dt3 = jnp.concatenate([dt_hi, dt_hi, dt_lo], axis=0)
        for b in range(5):
            here = pl.ds((2 * y + b) * BLOCK, BLOCK)
            dp = dot(vcat[here, :], dt3)
            hi, lo = split(s_ref[i, b] * (dp - row_dots))
            dscat[y, b * BLOCK : (b + 1) * BLOCK, h * 512 : h * 512 + 256] = hi
            dscat[y, b * BLOCK : (b + 1) * BLOCK, h * 512 + 256 : h * 512 + 512] = lo
        kts = kt[:, 2 * y * BLOCK : 2 * y * BLOCK + SPAN]
        both = dot(kts, dscat[y, :, h * 512 : h * 512 + 256])
        dq = both[:HEAD_DIM] + both[HEAD_DIM:] + dot(kts[:HEAD_DIM], dscat[y, :, h * 512 + 256 : h * 512 + 512])
        dq = dq * query_scale
        out_buf[8 * y : 8 * y + 8, 2 + h] = dq.T.reshape(8, ROWS, HEAD_DIM)

    def key_sums(y):
        for kind, cat, weight_ref in ((0, dscat, qw_ref), (1, wcat, dw_ref)):
            zero = jnp.zeros((BLOCK, HEAD_DIM), bf16)
            parts = []
            for h in range(2):
                both = weight_ref[y, h * BLOCK : (h + 1) * BLOCK, :]
                parts += [both, jnp.concatenate([both[:, :HEAD_DIM], zero], axis=1)]
            weights = jnp.concatenate(parts, axis=0)
            for b in range(5):
                both = dot(cat[y, b * BLOCK : (b + 1) * BLOCK, :], weights)
                part = both[:, :HEAD_DIM] + both[:, HEAD_DIM:]
                if kind == 0:
                    part = part * LN2
                r = 2 * y + b
                at = pl.ds(8 * (r // 2), 8) if r % 2 == 0 else pl.ds(pl.multiple_of(8 * (r // 2 + core), 8), 8)
                ref = gmine if r % 2 == 0 else gother
                part = part.reshape(8, ROWS, HEAD_DIM)
                if y == 1 and b < 3:
                    part = part + ref[at, kind]
                ref[at, kind] = part

    unused = pl.ds(pl.multiple_of(24 * (1 - core), 8), 8)
    gother[unused, :] = jnp.zeros((8, 2, ROWS, HEAD_DIM), f32)
    scores(0, 0)
    scores(0, 1)
    weigh(0, 0)
    scores(1, 0)
    weigh(0, 1)
    grads(0, 0)
    scores(1, 1)
    weigh(1, 0)
    grads(0, 1)
    key_sums(0)
    weigh(1, 1)
    grads(1, 0)
    grads(1, 1)
    key_sums(1)


def shape(*dims):
    return jax.ShapeDtypeStruct(dims, f32)


def call(kernel, outs, ins, scratch=(), cost=1, vmem=16):
    return pl.pallas_call(
        kernel,
        out_shape=outs,
        in_specs=[VMEM] * len(ins),
        out_specs=[VMEM] * len(outs) if isinstance(outs, tuple) else VMEM,
        scratch_shapes=list(scratch),
        compiler_params=params(vmem),
        cost_estimate=pl.CostEstimate(flops=cost * 1_000_000_000, bytes_accessed=cost * 3_000_000, transcendentals=0),
    )(*ins)


def exchanged(x):
    return lax.all_to_all(x, PLANE_AXES, 0, 0, tiled=True)


def swapped(x):
    return lax.ppermute(x, "core", [(0, 1), (1, 0)])


def attend_call(rows, own, halo, other):
    scratch = (
        pltpu.VMEM((7 * BLOCK, 3 * HEAD_DIM), bf16),
        pltpu.VMEM((7 * BLOCK, 3 * HEAD_DIM), bf16),
        pltpu.VMEM((2 * HEAD_DIM, 7 * BLOCK), bf16),
        pltpu.VMEM((2 * HEAD_DIM, 7 * BLOCK), bf16),
        pltpu.VMEM((4, 5, BLOCK, BLOCK), f32),
        pltpu.VMEM((2, SPAN, 4 * BLOCK), bf16),
        pltpu.VMEM((2, SPAN, 4 * BLOCK), bf16),
        pltpu.VMEM((2, 2 * BLOCK, 2 * HEAD_DIM), bf16),
        pltpu.VMEM((2, 2 * BLOCK, 2 * HEAD_DIM), bf16),
    )
    kv_shape = shape(2 * PEERS, 2, ROWS, HEAD_DIM)
    outs = (shape(PEERS, 4, ROWS, HEAD_DIM), kv_shape, kv_shape)
    return call(attend_kernel, outs, (rows, own, halo, other), scratch, cost=8, vmem=36)


def per_device(queries, keys, values, out_grad):
    planes = lax.axis_size("z")
    kv_shape = shape(PEERS, 2, ROWS, HEAD_DIM)
    q_shape = shape(PEERS, 4, ROWS, HEAD_DIM)
    own = exchanged(call(pack_kv_kernel, kv_shape, (keys, values), cost=1))
    packed = call(pack_q_kernel, q_shape, (queries, out_grad), cost=1)
    own, packed = lax.optimization_barrier((own, packed))
    rows = exchanged(packed)
    halo = lax.ppermute(own, "z", [(i, i + 1) for i in range(planes - 1)])
    ownx = swapped(own)
    halox = swapped(halo)
    half = PEERS // 2
    rows, ownx, halox = lax.optimization_barrier((rows, ownx, halox))
    other = jnp.where(
        lax.axis_index("core") == 0,
        jnp.concatenate([halox, ownx[:half]], axis=0),
        jnp.concatenate([halox[half:], ownx], axis=0),
    )
    out, gmine, gother = attend_call(rows, own, halo, other)
    back = exchanged(out)
    received = swapped(gother)
    ghalo = gmine[:PEERS] + received[:PEERS]
    returned = lax.ppermute(ghalo, "z", [(i + 1, i) for i in range(planes - 1)])
    total = gmine[PEERS:] + received[PEERS:] + returned
    kv_back = exchanged(total)
    attention, query_grad = call(unpack_q_kernel, (shape(ROWS, HEADS, HEAD_DIM),) * 2, (back,), cost=1)
    key_grad, value_grad = call(unpack_kv_kernel, (shape(ROWS, GROUPS, HEAD_DIM),) * 2, (kv_back,), cost=1)
    return attention, query_grad, key_grad, value_grad


def solution(mesh):
    inner = Mesh(mesh.devices.reshape(-1, 2, 2, mesh.shape["head"]), ("z", "ylo", "core", "head"))
    spec = P(("z", "ylo", "core", "head"), None, None)
    return jax.shard_map(per_device, mesh=inner, in_specs=(spec,) * 4, out_specs=(spec,) * 4, check_vma=False)
```

```python
import jax
import jax.numpy as jnp
from jax import lax
from jax.experimental import pallas as pl
from jax.experimental.pallas import tpu as pltpu
from jax.sharding import Mesh, PartitionSpec as P

WINDOW = 1024
HEADS = 32
GROUPS = 16
HEAD_DIM = 128
ROWS = 32
BLOCK = 256
PEERS = 16
PLANE_AXES = ("ylo", "head")

query_scale = 168.0 ** (-0.5)
LOG2E = 1.4426950408889634
LN2 = 0.6931471805599453
f32 = jnp.float32
bf16 = jnp.bfloat16

VMEM = pl.BlockSpec(memory_space=pltpu.VMEM)


def params(vmem):
    return pltpu.CompilerParams(vmem_limit_bytes=vmem * 1024 * 1024)


def pack_kv_kernel(k_ref, v_ref, out_ref):
    for g in range(GROUPS):
        out_ref[g, 0] = k_ref[:, g, :]
        out_ref[g, 1] = v_ref[:, g, :]


def pack_q_kernel(q_ref, d_ref, out_ref):
    for g in range(GROUPS):
        for h in range(2):
            out_ref[g, h] = q_ref[:, 2 * g + h, :]
            out_ref[g, 2 + h] = d_ref[:, 2 * g + h, :]


def unpack_kv_kernel(in_ref, k_ref, v_ref):
    for g in range(GROUPS):
        k_ref[:, g, :] = in_ref[g, 0]
        v_ref[:, g, :] = in_ref[g, 1]


def unpack_q_kernel(in_ref, a_ref, q_ref):
    for g in range(GROUPS):
        for h in range(2):
            a_ref[:, 2 * g + h, :] = in_ref[g, h]
            q_ref[:, 2 * g + h, :] = in_ref[g, 2 + h]


def split(x):
    hi = x.astype(bf16)
    lo = (x - hi.astype(f32)).astype(bf16)
    return hi, lo


def dot(a, b):
    return lax.dot_general(a, b, (((1,), (0,)), ((), ())), preferred_element_type=f32)


SPAN = 5 * BLOCK


def attend_kernel(
    rows_in, own_in, halo_in, other_in,
    out_buf, gmine, gother,
    kcat, vcat, kt, vt, s_ref, wcat, dscat, qw_ref, dw_ref,
):
    z = lax.axis_index("z")
    core = lax.axis_index("core")
    for r in range(7):
        here = pl.ds(r * BLOCK, BLOCK)
        for i, cat, tr in ((0, kcat, kt), (1, vcat, vt)):
            ref, at = (other_in, 8 * (r // 2)) if r % 2 else (halo_in if r < 4 else own_in, 8 * (r // 2 % 2))
            x = ref[at : at + 8, i]
            x = x.reshape(BLOCK, HEAD_DIM)
            hi, lo = split(x)
            cat[here, :HEAD_DIM] = hi
            cat[here, HEAD_DIM : 2 * HEAD_DIM] = lo
            cat[here, 2 * HEAD_DIM :] = hi
            thi, tlo = split(x.T)
            tr[:HEAD_DIM, here] = thi
            tr[HEAD_DIM:, here] = tlo
    key_iota = lax.broadcasted_iota(jnp.int32, (BLOCK, BLOCK), 0)
    query_iota = lax.broadcasted_iota(jnp.int32, (BLOCK, BLOCK), 1)
    later = key_iota > query_iota

    def exists(y, b):
        return (z * 4 + 2 * y + core + b - 4) >= 0

    state = {}

    def scores(y, h):
        q = rows_in[8 * y : 8 * y + 8, h].reshape(BLOCK, HEAD_DIM) * (query_scale * LOG2E)
        qt_hi, qt_lo = split(q.T)
        q_hi, q_lo = split(q)
        qt3 = jnp.concatenate([qt_hi, qt_hi, qt_lo], axis=0)
        row_max = None
        for b in range(5):
            here = pl.ds((2 * y + b) * BLOCK, BLOCK)
            s = dot(kcat[here, :], qt3)
            if b == 0:
                s = jnp.where(later, s, -jnp.inf)
            if b == 4:
                s = jnp.where(later, -jnp.inf, s)
            s_ref[2 * y + h, b] = s
            m = jnp.max(s, axis=0, keepdims=True)
            if b < 4:
                m = jnp.where(exists(y, b), m, -jnp.inf)
            row_max = m if row_max is None else jnp.maximum(row_max, m)
        qw_ref[y, h * BLOCK : (h + 1) * BLOCK, :] = jnp.concatenate([q_hi, q_lo], axis=1)
        state[y, h] = row_max

    def weigh(y, h):
        row_max = state[y, h]
        i = 2 * y + h
        total = None
        for b in range(5):
            shift = row_max if b == 4 else jnp.where(exists(y, b), row_max, jnp.inf)
            w = jnp.exp2(s_ref[i, b] - shift)
            t = jnp.sum(w, axis=0, keepdims=True)
            total = t if total is None else total + t
            hi, lo = split(w)
            s_ref[i, b] = w
            wcat[y, b * BLOCK : (b + 1) * BLOCK, h * 512 : h * 512 + 256] = hi
            wcat[y, b * BLOCK : (b + 1) * BLOCK, h * 512 + 256 : h * 512 + 512] = lo
        vts = vt[:, 2 * y * BLOCK : 2 * y * BLOCK + SPAN]
        both = dot(vts, wcat[y, :, h * 512 : h * 512 + 256])
        at_sum = both[:HEAD_DIM] + both[HEAD_DIM:] + dot(vts[:HEAD_DIM], wcat[y, :, h * 512 + 256 : h * 512 + 512])
        inverse = 1.0 / total
        at_sum = at_sum * inverse
        out_buf[8 * y : 8 * y + 8, h] = at_sum.T.reshape(8, ROWS, HEAD_DIM)
        dt = rows_in[8 * y : 8 * y + 8, 2 + h].reshape(BLOCK, HEAD_DIM).T * inverse
        row_dots = jnp.sum(dt * at_sum, axis=0, keepdims=True)
        d_hi, d_lo = split(dt.T)
        dw_ref[y, h * BLOCK : (h + 1) * BLOCK, :] = jnp.concatenate([d_hi, d_lo], axis=1)
        state[y, h] = (row_dots, dt)

    def grads(y, h):
        row_dots, dt = state[y, h]
        i = 2 * y + h
        dt_hi, dt_lo = split(dt)
        dt3 = jnp.concatenate([dt_hi, dt_hi, dt_lo], axis=0)
        for b in range(5):
            here = pl.ds((2 * y + b) * BLOCK, BLOCK)
            dp = dot(vcat[here, :], dt3)
            hi, lo = split(s_ref[i, b] * (dp - row_dots))
            dscat[y, b * BLOCK : (b + 1) * BLOCK, h * 512 : h * 512 + 256] = hi
            dscat[y, b * BLOCK : (b + 1) * BLOCK, h * 512 + 256 : h * 512 + 512] = lo
        kts = kt[:, 2 * y * BLOCK : 2 * y * BLOCK + SPAN]
        both = dot(kts, dscat[y, :, h * 512 : h * 512 + 256])
        dq = both[:HEAD_DIM] + both[HEAD_DIM:] + dot(kts[:HEAD_DIM], dscat[y, :, h * 512 + 256 : h * 512 + 512])
        dq = dq * query_scale
        out_buf[8 * y : 8 * y + 8, 2 + h] = dq.T.reshape(8, ROWS, HEAD_DIM)

    def key_sums(y):
        for kind, cat, weight_ref in ((0, dscat, qw_ref), (1, wcat, dw_ref)):
            zero = jnp.zeros((BLOCK, HEAD_DIM), bf16)
            parts = []
            for h in range(2):
                both = weight_ref[y, h * BLOCK : (h + 1) * BLOCK, :]
                parts += [both, jnp.concatenate([both[:, :HEAD_DIM], zero], axis=1)]
            weights = jnp.concatenate(parts, axis=0)
            for b in range(5):
                both = dot(cat[y, b * BLOCK : (b + 1) * BLOCK, :], weights)
                part = both[:, :HEAD_DIM] + both[:, HEAD_DIM:]
                if kind == 0:
                    part = part * LN2
                r = 2 * y + b
                at = pl.ds(8 * (r // 2), 8) if r % 2 == 0 else pl.ds(pl.multiple_of(8 * (r // 2 + core), 8), 8)
                ref = gmine if r % 2 == 0 else gother
                part = part.reshape(8, ROWS, HEAD_DIM)
                if y == 1 and b < 3:
                    part = part + ref[at, kind]
                ref[at, kind] = part

    unused = pl.ds(pl.multiple_of(24 * (1 - core), 8), 8)
    gother[unused, :] = jnp.zeros((8, 2, ROWS, HEAD_DIM), f32)
    scores(0, 0)
    scores(0, 1)
    weigh(0, 0)
    scores(1, 0)
    weigh(0, 1)
    grads(0, 0)
    scores(1, 1)
    weigh(1, 0)
    grads(0, 1)
    key_sums(0)
    weigh(1, 1)
    grads(1, 0)
    grads(1, 1)
    key_sums(1)


def shape(*dims):
    return jax.ShapeDtypeStruct(dims, f32)


def call(kernel, outs, ins, scratch=(), cost=1, vmem=16):
    return pl.pallas_call(
        kernel,
        out_shape=outs,
        in_specs=[VMEM] * len(ins),
        out_specs=[VMEM] * len(outs) if isinstance(outs, tuple) else VMEM,
        scratch_shapes=list(scratch),
        compiler_params=params(vmem),
        cost_estimate=pl.CostEstimate(flops=cost * 1_000_000_000, bytes_accessed=cost * 3_000_000, transcendentals=0),
    )(*ins)


def exchanged(x):
    return lax.all_to_all(x, PLANE_AXES, 0, 0, tiled=True)


def swapped(x):
    return lax.ppermute(x, "core", [(0, 1), (1, 0)])


def attend_call(rows, own, halo, other):
    scratch = (
        pltpu.VMEM((7 * BLOCK, 3 * HEAD_DIM), bf16),
        pltpu.VMEM((7 * BLOCK, 3 * HEAD_DIM), bf16),
        pltpu.VMEM((2 * HEAD_DIM, 7 * BLOCK), bf16),
        pltpu.VMEM((2 * HEAD_DIM, 7 * BLOCK), bf16),
        pltpu.VMEM((4, 5, BLOCK, BLOCK), f32),
        pltpu.VMEM((2, SPAN, 4 * BLOCK), bf16),
        pltpu.VMEM((2, SPAN, 4 * BLOCK), bf16),
        pltpu.VMEM((2, 2 * BLOCK, 2 * HEAD_DIM), bf16),
        pltpu.VMEM((2, 2 * BLOCK, 2 * HEAD_DIM), bf16),
    )
    kv_shape = shape(2 * PEERS, 2, ROWS, HEAD_DIM)
    outs = (shape(PEERS, 4, ROWS, HEAD_DIM), kv_shape, kv_shape)
    return call(attend_kernel, outs, (rows, own, halo, other), scratch, cost=8, vmem=36)


def per_device(queries, keys, values, out_grad):
    planes = lax.axis_size("z")
    kv_shape = shape(PEERS, 2, ROWS, HEAD_DIM)
    q_shape = shape(PEERS, 4, ROWS, HEAD_DIM)
    own = exchanged(call(pack_kv_kernel, kv_shape, (keys, values), cost=1, vmem=60))
    packed = call(pack_q_kernel, q_shape, (queries, out_grad), cost=1)
    own, packed = lax.optimization_barrier((own, packed))
    rows = exchanged(packed)
    halo = lax.ppermute(own, "z", [(i, i + 1) for i in range(planes - 1)])
    ownx = swapped(own)
    halox = swapped(halo)
    half = PEERS // 2
    rows, ownx, halox = lax.optimization_barrier((rows, ownx, halox))
    other = jnp.where(
        lax.axis_index("core") == 0,
        jnp.concatenate([halox, ownx[:half]], axis=0),
        jnp.concatenate([halox[half:], ownx], axis=0),
    )
    out, gmine, gother = attend_call(rows, own, halo, other)
    back = exchanged(out)
    received = swapped(gother)
    ghalo = gmine[:PEERS] + received[:PEERS]
    returned = lax.ppermute(ghalo, "z", [(i + 1, i) for i in range(planes - 1)])
    total = gmine[PEERS:] + received[PEERS:] + returned
    kv_back = exchanged(total)
    attention, query_grad = call(unpack_q_kernel, (shape(ROWS, HEADS, HEAD_DIM),) * 2, (back,), cost=1)
    key_grad, value_grad = call(unpack_kv_kernel, (shape(ROWS, GROUPS, HEAD_DIM),) * 2, (kv_back,), cost=1)
    return attention, query_grad, key_grad, value_grad


def solution(mesh):
    inner = Mesh(mesh.devices.reshape(-1, 2, 2, mesh.shape["head"]), ("z", "ylo", "core", "head"))
    spec = P(("z", "ylo", "core", "head"), None, None)
    return jax.shard_map(per_device, mesh=inner, in_specs=(spec,) * 4, out_specs=(spec,) * 4, check_vma=False)
```

```python
import jax
import jax.numpy as jnp
from jax import lax
from jax.experimental import pallas as pl
from jax.experimental.pallas import tpu as pltpu
from jax.sharding import Mesh, PartitionSpec as P

WINDOW = 1024
HEADS = 32
GROUPS = 16
HEAD_DIM = 128
ROWS = 32
BLOCK = 256
PEERS = 16
PLANE_AXES = ("ylo", "head")

query_scale = 168.0 ** (-0.5)
LOG2E = 1.4426950408889634
LN2 = 0.6931471805599453
f32 = jnp.float32
bf16 = jnp.bfloat16

VMEM = pl.BlockSpec(memory_space=pltpu.VMEM)


def params(vmem):
    return pltpu.CompilerParams(vmem_limit_bytes=vmem * 1024 * 1024)


def pack_kv_kernel(k_ref, v_ref, out_ref):
    for g in range(GROUPS // 2):
        out_ref[g, 0] = k_ref[:, g, :]
        out_ref[g, 1] = v_ref[:, g, :]


def pack_kv_call(keys, values):
    half = GROUPS // 2
    heads = pl.BlockSpec((ROWS, half, HEAD_DIM), lambda i: (0, i, 0))
    return pl.pallas_call(
        pack_kv_kernel,
        out_shape=shape(PEERS, 2, ROWS, HEAD_DIM),
        grid=(2,),
        in_specs=[heads, heads],
        out_specs=pl.BlockSpec((half, 2, ROWS, HEAD_DIM), lambda i: (i, 0, 0, 0)),
        compiler_params=params(60),
    )(keys, values)


def pack_q_kernel(q_ref, d_ref, out_ref):
    for g in range(GROUPS):
        for h in range(2):
            out_ref[g, h] = q_ref[:, 2 * g + h, :]
            out_ref[g, 2 + h] = d_ref[:, 2 * g + h, :]


def unpack_kv_kernel(in_ref, k_ref, v_ref):
    for g in range(GROUPS):
        k_ref[:, g, :] = in_ref[g, 0]
        v_ref[:, g, :] = in_ref[g, 1]


def unpack_q_kernel(in_ref, a_ref, q_ref):
    for g in range(GROUPS):
        for h in range(2):
            a_ref[:, 2 * g + h, :] = in_ref[g, h]
            q_ref[:, 2 * g + h, :] = in_ref[g, 2 + h]


def split(x):
    hi = x.astype(bf16)
    lo = (x - hi.astype(f32)).astype(bf16)
    return hi, lo


def dot(a, b):
    return lax.dot_general(a, b, (((1,), (0,)), ((), ())), preferred_element_type=f32)


SPAN = 5 * BLOCK


def attend_kernel(
    rows_in, own_in, halo_in, other_in,
    out_buf, gmine, gother,
    kcat, vcat, kt, vt, s_ref, wcat, dscat, qw_ref, dw_ref,
):
    z = lax.axis_index("z")
    core = lax.axis_index("core")
    def prepare(i, blocks):
        cat, tr = ((kcat, kt), (vcat, vt))[i]
        for r in blocks:
            here = pl.ds(r * BLOCK, BLOCK)
            ref, at = (other_in, 8 * (r // 2)) if r % 2 else (halo_in if r < 4 else own_in, 8 * (r // 2 % 2))
            x = ref[at : at + 8, i].reshape(BLOCK, HEAD_DIM)
            hi, lo = split(x)
            cat[here, :HEAD_DIM] = hi
            cat[here, HEAD_DIM : 2 * HEAD_DIM] = lo
            cat[here, 2 * HEAD_DIM :] = hi
            thi, tlo = split(x.T)
            tr[:HEAD_DIM, here] = thi
            tr[HEAD_DIM:, here] = tlo

    key_iota = lax.broadcasted_iota(jnp.int32, (BLOCK, BLOCK), 0)
    query_iota = lax.broadcasted_iota(jnp.int32, (BLOCK, BLOCK), 1)
    later = key_iota > query_iota

    def exists(y, b):
        return (z * 4 + 2 * y + core + b - 4) >= 0

    state = {}

    def scores(y, h):
        q = rows_in[8 * y : 8 * y + 8, h].reshape(BLOCK, HEAD_DIM) * (query_scale * LOG2E)
        qt_hi, qt_lo = split(q.T)
        q_hi, q_lo = split(q)
        qt3 = jnp.concatenate([qt_hi, qt_hi, qt_lo], axis=0)
        row_max = None
        for b in range(5):
            here = pl.ds((2 * y + b) * BLOCK, BLOCK)
            s = dot(kcat[here, :], qt3)
            if b == 0:
                s = jnp.where(later, s, -jnp.inf)
            if b == 4:
                s = jnp.where(later, -jnp.inf, s)
            s_ref[2 * y + h, b] = s
            m = jnp.max(s, axis=0, keepdims=True)
            if b < 4:
                m = jnp.where(exists(y, b), m, -jnp.inf)
            row_max = m if row_max is None else jnp.maximum(row_max, m)
            yield
        qw_ref[y, h * BLOCK : (h + 1) * BLOCK, :] = jnp.concatenate([q_hi, q_lo], axis=1)
        state[y, h] = row_max

    def weigh(y, h):
        row_max = state[y, h]
        i = 2 * y + h
        total = None
        for b in range(5):
            shift = row_max if b == 4 else jnp.where(exists(y, b), row_max, jnp.inf)
            w = jnp.exp2(s_ref[i, b] - shift)
            t = jnp.sum(w, axis=0, keepdims=True)
            total = t if total is None else total + t
            hi, lo = split(w)
            s_ref[i, b] = w
            wcat[y, b * BLOCK : (b + 1) * BLOCK, h * 512 : h * 512 + 256] = hi
            wcat[y, b * BLOCK : (b + 1) * BLOCK, h * 512 + 256 : h * 512 + 512] = lo
            yield
        vts = vt[:, 2 * y * BLOCK : 2 * y * BLOCK + SPAN]
        both = dot(vts, wcat[y, :, h * 512 : h * 512 + 256])
        at_sum = both[:HEAD_DIM] + both[HEAD_DIM:] + dot(vts[:HEAD_DIM], wcat[y, :, h * 512 + 256 : h * 512 + 512])
        inverse = 1.0 / total
        at_sum = at_sum * inverse
        out_buf[8 * y : 8 * y + 8, h] = at_sum.T.reshape(8, ROWS, HEAD_DIM)
        dt = rows_in[8 * y : 8 * y + 8, 2 + h].reshape(BLOCK, HEAD_DIM).T * inverse
        row_dots = jnp.sum(dt * at_sum, axis=0, keepdims=True)
        d_hi, d_lo = split(dt.T)
        dw_ref[y, h * BLOCK : (h + 1) * BLOCK, :] = jnp.concatenate([d_hi, d_lo], axis=1)
        state[y, h] = (row_dots, dt)

    def grads(y, h):
        row_dots, dt = state[y, h]
        i = 2 * y + h
        dt_hi, dt_lo = split(dt)
        dt3 = jnp.concatenate([dt_hi, dt_hi, dt_lo], axis=0)
        for b in range(5):
            here = pl.ds((2 * y + b) * BLOCK, BLOCK)
            dp = dot(vcat[here, :], dt3)
            hi, lo = split(s_ref[i, b] * (dp - row_dots))
            dscat[y, b * BLOCK : (b + 1) * BLOCK, h * 512 : h * 512 + 256] = hi
            dscat[y, b * BLOCK : (b + 1) * BLOCK, h * 512 + 256 : h * 512 + 512] = lo
            yield
        kts = kt[:, 2 * y * BLOCK : 2 * y * BLOCK + SPAN]
        both = dot(kts, dscat[y, :, h * 512 : h * 512 + 256])
        dq = both[:HEAD_DIM] + both[HEAD_DIM:] + dot(kts[:HEAD_DIM], dscat[y, :, h * 512 + 256 : h * 512 + 512])
        dq = dq * query_scale
        out_buf[8 * y : 8 * y + 8, 2 + h] = dq.T.reshape(8, ROWS, HEAD_DIM)

    def key_sums(y, kind):
        cat, weight_ref = ((dscat, qw_ref), (wcat, dw_ref))[kind]
        zero = jnp.zeros((BLOCK, HEAD_DIM), bf16)
        parts = []
        for h in range(2):
            both = weight_ref[y, h * BLOCK : (h + 1) * BLOCK, :]
            parts += [both, jnp.concatenate([both[:, :HEAD_DIM], zero], axis=1)]
        weights = jnp.concatenate(parts, axis=0)
        for b in range(5):
            both = dot(cat[y, b * BLOCK : (b + 1) * BLOCK, :], weights)
            part = both[:, :HEAD_DIM] + both[:, HEAD_DIM:]
            if kind == 0:
                part = part * LN2
            r = 2 * y + b
            at = pl.ds(8 * (r // 2), 8) if r % 2 == 0 else pl.ds(pl.multiple_of(8 * (r // 2 + core), 8), 8)
            ref = gmine if r % 2 == 0 else gother
            part = part.reshape(8, ROWS, HEAD_DIM)
            if y == 1 and b < 3:
                part = part + ref[at, kind]
            ref[at, kind] = part
            yield

    def run(*stages):
        stages = list(stages)
        while stages:
            for stage in list(stages):
                if next(stage, stage) is stage:
                    stages.remove(stage)

    unused = pl.ds(pl.multiple_of(24 * (1 - core), 8), 8)
    gother[unused, :] = jnp.zeros((8, 2, ROWS, HEAD_DIM), f32)
    prepare(0, range(7))
    prepare(1, range(7))
    run(scores(0, 0))
    run(scores(0, 1))
    run(weigh(0, 0), scores(1, 0))
    run(weigh(0, 1), scores(1, 1))
    run(grads(0, 0), weigh(1, 0))
    run(grads(0, 1), weigh(1, 1))
    run(grads(1, 0), key_sums(0, 1))
    run(grads(1, 1), key_sums(0, 0))
    run(key_sums(1, 1))
    run(key_sums(1, 0))


def shape(*dims):
    return jax.ShapeDtypeStruct(dims, f32)


def call(kernel, outs, ins, scratch=(), cost=1, vmem=16):
    return pl.pallas_call(
        kernel,
        out_shape=outs,
        in_specs=[VMEM] * len(ins),
        out_specs=[VMEM] * len(outs) if isinstance(outs, tuple) else VMEM,
        scratch_shapes=list(scratch),
        compiler_params=params(vmem),
        cost_estimate=pl.CostEstimate(flops=cost * 1_000_000_000, bytes_accessed=cost * 3_000_000, transcendentals=0),
    )(*ins)


def exchanged(x):
    return lax.all_to_all(x, PLANE_AXES, 0, 0, tiled=True)


def swapped(x):
    return lax.ppermute(x, "core", [(0, 1), (1, 0)])


def attend_call(rows, own, halo, other):
    scratch = (
        pltpu.VMEM((7 * BLOCK, 3 * HEAD_DIM), bf16),
        pltpu.VMEM((7 * BLOCK, 3 * HEAD_DIM), bf16),
        pltpu.VMEM((2 * HEAD_DIM, 7 * BLOCK), bf16),
        pltpu.VMEM((2 * HEAD_DIM, 7 * BLOCK), bf16),
        pltpu.VMEM((4, 5, BLOCK, BLOCK), f32),
        pltpu.VMEM((2, SPAN, 4 * BLOCK), bf16),
        pltpu.VMEM((2, SPAN, 4 * BLOCK), bf16),
        pltpu.VMEM((2, 2 * BLOCK, 2 * HEAD_DIM), bf16),
        pltpu.VMEM((2, 2 * BLOCK, 2 * HEAD_DIM), bf16),
    )
    kv_shape = shape(2 * PEERS, 2, ROWS, HEAD_DIM)
    outs = (shape(PEERS, 4, ROWS, HEAD_DIM), kv_shape, kv_shape)
    return call(attend_kernel, outs, (rows, own, halo, other), scratch, cost=8, vmem=36)


def per_device(queries, keys, values, out_grad):
    planes = lax.axis_size("z")
    kv_shape = shape(PEERS, 2, ROWS, HEAD_DIM)
    q_shape = shape(PEERS, 4, ROWS, HEAD_DIM)
    own = exchanged(pack_kv_call(keys, values))
    packed = call(pack_q_kernel, q_shape, (queries, out_grad), cost=1)
    own, packed = lax.optimization_barrier((own, packed))
    rows = exchanged(packed)
    halo = lax.ppermute(own, "z", [(i, i + 1) for i in range(planes - 1)])
    ownx = swapped(own)
    halox = swapped(halo)
    half = PEERS // 2
    rows, ownx, halox = lax.optimization_barrier((rows, ownx, halox))
    other = jnp.where(
        lax.axis_index("core") == 0,
        jnp.concatenate([halox, ownx[:half]], axis=0),
        jnp.concatenate([halox[half:], ownx], axis=0),
    )
    out, gmine, gother = attend_call(rows, own, halo, other)
    back = exchanged(out)
    received = swapped(gother)
    ghalo = gmine[:PEERS] + received[:PEERS]
    returned = lax.ppermute(ghalo, "z", [(i + 1, i) for i in range(planes - 1)])
    total = gmine[PEERS:] + received[PEERS:] + returned
    kv_back = exchanged(total)
    attention, query_grad = call(unpack_q_kernel, (shape(ROWS, HEADS, HEAD_DIM),) * 2, (back,), cost=1)
    key_grad, value_grad = call(unpack_kv_kernel, (shape(ROWS, GROUPS, HEAD_DIM),) * 2, (kv_back,), cost=1)
    return attention, query_grad, key_grad, value_grad


def solution(mesh):
    inner = Mesh(mesh.devices.reshape(-1, 2, 2, mesh.shape["head"]), ("z", "ylo", "core", "head"))
    spec = P(("z", "ylo", "core", "head"), None, None)
    return jax.shard_map(per_device, mesh=inner, in_specs=(spec,) * 4, out_specs=(spec,) * 4, check_vma=False)
```
